512 devices in a mesh: req: 4 (over x), head: 2 (over core), exp: 64 (over z, y).
Axes of the slice: x: 4, y: 8, z: 8, core: 2. Of those that a mesh axis runs over, the one named last changes fastest.
Arguments:
- hidden_acts: bfloat16 [65536, 6, 768], P(('req', 'exp'), None, 'head'), parts along dimension 0, may hold values from -6 to 6
- picks: int32 [65536, 6], P(('req', 'exp')), parts along dimension 0, may hold values from 0 to 127, all different within a row; in each aligned block of 256 rows (0 to 255, 256 to 511, ...) at most 15 rows name the same one
- levels: int32 [65536, 6], P(('req', 'exp')), parts along dimension 0, may hold values from 1 to 1024
- down_weight: bfloat16 [128, 768, 2560], P('exp', None, 'head'), may hold values from -0.21875 to 0.21875
Outputs:
- combined: bfloat16 [65536, 2560], P(('req', 'exp'), 'head'), parts along dimension 0
The draws below stay inside these ranges and needn't reach their ends.
There are 4 independent parts, one for each index of `req`. The reference program is written for one: setup_inputs(seed, part) draws one part's arguments, and reference() takes and returns one part's arrays. A program takes and returns all parts, laid end to end along the dimension named above; an argument that names none is the same for every part. Nothing has to cross between parts.
Inputs may be any that keep to these rules, and one draw needn't show every extreme that they name: `picks`: each row names 6 different experts. In each aligned block of 256 rows (the rows of one device) no expert is named by more than 15 rows; in some block one expert is named by exactly 15.
All inputs are finite; a program needn't handle non-finite values.
Results may differ from the reference program's by a relative error of at most 0.0049.
Values may be sent and summed in bfloat16 or wider, within the bound.
No kernel may reach another device: no remote copies, remote signals or barrier semaphores. Data moves between devices by JAX's collectives and lax.ppermute only.
A program may use at most 64 MiB of HBM per device.

```python
import math
import jax
import jax.numpy as jnp
import numpy as np
from jax import lax

D = 2560
H = 768
TOP = 6
TOK_DEV = 256
EXPERTS = 128
CAP = 15
TOKENS = 16384
N_EXP = 64


def place_ends(entries, own_key, smallest, largest):
    longest = entries.shape.index(max(entries.shape))
    spots = []
    for shift in (0, 1):
        where = [jax.random.randint(jax.random.fold_in(own_key, axis), (), 0, length) for axis, length in enumerate(entries.shape)]
        where[longest] = (where[longest] + shift) % entries.shape[longest]
        spots.append(tuple(where))
    return entries.at[spots[0]].set(smallest).at[spots[1]].set(largest)


def block_scale(own_key, extent, split, low, high):
    def one(axis_at, blocks):
        heights = jax.random.uniform(jax.random.fold_in(jax.random.fold_in(own_key, 6), axis_at), (blocks,), jnp.float32, low / len(split), high / len(split))
        return jnp.repeat(jnp.exp(heights), extent[axis_at] // blocks).reshape((-1,) + (1,) * (len(extent) - axis_at - 1))

    loudness = one(*split[0])
    for cut in split[1:]:
        loudness = loudness * one(*cut)
    return loudness


def shared_out(stream_key, own, number, rows, count, top, limit, slope):
    sequence = jax.random.permutation(stream_key, count)
    packed, ordinary = load_shares(count, rows * top, limit, slope, True), load_shares(count, rows * top, limit, slope, False)
    places = jnp.arange(count)

    def named(lengths, rotation):
        used = int((lengths > 0).sum())
        fixed = max(1, used // 4)
        passed = fixed + (places - fixed + rotation * (used - fixed)) % max(1, count - fixed)
        return jnp.zeros((count,), jnp.int32).at[sequence[jnp.where(places < fixed, places, passed)]].set(jnp.asarray(lengths, jnp.int32))

    lengths = jnp.where(number % 4 == 0, named(packed, number // 4), named(ordinary, number - number // 4 - 1))
    mixed = jax.random.permutation(jax.random.fold_in(own, 3), count)
    source_of, taker = mixed[0:count // 2 * 2:2], mixed[1:count // 2 * 2:2]
    margin = jnp.minimum(lengths[source_of] - 1, limit - lengths[taker]) // 2
    margin = jnp.where((source_of == sequence[0]) | (taker == sequence[0]) | (lengths[taker] == 0), 0, jnp.maximum(margin, 0))
    passed = jax.random.randint(jax.random.fold_in(own, 4), (count // 2,), 0, 1 << 20) % (margin + 1)
    lengths = lengths.at[source_of].add(-passed).at[taker].add(passed)
    labels = jnp.searchsorted(jnp.cumsum(lengths), jnp.arange(rows * top), side="right").astype(jnp.int32)
    grid = labels.reshape(top, rows).T
    grid = grid[jax.random.permutation(jax.random.fold_in(own, 1), rows)]
    rotation = jax.random.randint(jax.random.fold_in(own, 2), (rows, 1), 0, top)
    return jnp.take_along_axis(grid, (jnp.arange(top)[None, :] + rotation) % top, axis=1)


def load_shares(amount, total, reach, slope, full):
    loads = [(1 << 20) // math.isqrt(grade ** slope) + 1 for grade in range(1, amount + 1)]
    largest = reach if full else min(reach, max(-(-total // amount), total * loads[0] // sum(loads)))
    least = 1 if total - largest >= amount - 1 else 0
    holding, spare = [largest] + [least] * (amount - 1), total - largest - least * (amount - 1)
    while spare > 0:
        free = [i for i in range(1, amount) if holding[i] < largest] or [i for i in range(1, amount) if holding[i] < reach]
        pool, left = sum([loads[i] for i in free]), spare
        for i in free:
            more = min(reach - holding[i], max(1, left * loads[i] // pool), spare)
            holding[i] = holding[i] + more
            spare = spare - more
    return np.array(holding)


def noise(key, extent, spread, reach, split=(), kind=jnp.bfloat16):
    drawn = jax.random.normal(key, extent, jnp.float32) * spread
    if len(split) > 0:
        drawn = block_scale(key, extent, split, -0.22, 0.18) * drawn
    return jnp.clip(drawn, min=-reach, max=reach).astype(kind)


def setup_inputs(seed: int = 0, part: int = 0) -> dict:
    key_of = jax.random.split(jax.random.key(seed), 5)
    own_keys = jax.random.split(jax.random.fold_in(key_of[4], part), 5)
    hidden_acts = noise(own_keys[0], (TOKENS, TOP, H), 1.0, 6.0, ((0, 64), (2, 2)))
    picks_keys = jax.random.split(jax.random.fold_in(own_keys[1], 1), TOKENS // TOK_DEV)
    picks_turns = jax.random.permutation(jax.random.fold_in(own_keys[1], 3), TOKENS // TOK_DEV)
    picks = jax.vmap(lambda own, number: shared_out(jax.random.fold_in(own_keys[1], 2), own, number, TOK_DEV, EXPERTS, TOP, CAP, 2))(picks_keys, picks_turns).reshape((TOKENS, TOP))
    levels = place_ends(jax.random.randint(own_keys[2], (TOKENS, TOP), 1, 1025), jax.random.fold_in(own_keys[2], 1), 1, 1024).astype(jnp.int32)
    down_weight = noise(key_of[3], (EXPERTS, H, D), H ** -0.5, 0.21875, ((0, 64), (2, 2)))
    return dict(hidden_acts=hidden_acts, picks=picks, levels=levels, down_weight=down_weight)


def apply_expert(pair):
    return jnp.dot(pair[0], pair[1], preferred_element_type=jnp.float32).astype(jnp.bfloat16)


def reference(hidden_acts, picks, levels, down_weight):
    block_picks = picks.reshape(N_EXP, TOK_DEV * TOP)
    onehot = (block_picks[:, :, None] == jnp.arange(EXPERTS, dtype=jnp.int32)[None, None, :]).astype(jnp.int32)
    earlier = jnp.cumsum(onehot, axis=1) - onehot
    slot_index = jnp.sum(earlier * onehot, axis=2).astype(jnp.int32)
    source = jnp.arange(N_EXP, dtype=jnp.int32)[:, None]
    target = (block_picks * (N_EXP * CAP) + source * CAP + slot_index).reshape(-1).astype(jnp.int32)
    hidden_width = hidden_acts.shape[2]
    buffer = jnp.zeros((EXPERTS * N_EXP * CAP, hidden_width), jnp.bfloat16)
    buffer = buffer.at[target].set(hidden_acts.reshape(-1, hidden_width))
    buffer = buffer.reshape(EXPERTS, N_EXP * CAP, hidden_width)
    produced = lax.map(apply_expert, (buffer, down_weight))
    back_rows = produced.reshape(EXPERTS * N_EXP * CAP, -1)[target]
    pick_weight = levels.astype(jnp.float32) / 1024.0
    summed = jnp.sum(back_rows.reshape(TOKENS, TOP, -1).astype(jnp.float32) * pick_weight[:, :, None], axis=1)
    return summed.astype(jnp.bfloat16)
```

```python
import functools

import jax
import jax.numpy as jnp
from jax import lax
from jax.experimental import pallas as pl
from jax.experimental.pallas import tpu as pltpu
from jax.sharding import PartitionSpec as P

WIDE = 8
SLOTS = 16
VMEM = 48 * 1024 * 1024


def route_kernel(pick_ref, hidden_ref, rows_ref, target_ref, *, experts):
    top, tokens = pick_ref.shape
    before = lax.broadcasted_iota(jnp.int32, (tokens, tokens), 0)
    after = lax.broadcasted_iota(jnp.int32, (tokens, tokens), 1)
    earlier = jnp.where(before < after, 1.0, 0.0).astype(jnp.bfloat16)
    named = lax.broadcasted_iota(jnp.int32, (experts, tokens), 0)
    carry = jnp.zeros((experts, 1), jnp.float32)
    target_ref[...] = jnp.full(target_ref.shape, -1, jnp.int32)
    targets = []
    for k in range(top):
        pick = pick_ref[k : k + 1, :]
        onehot = jnp.where(named == pick, 1.0, 0.0)
        count = jnp.dot(
            onehot.astype(jnp.bfloat16), earlier, preferred_element_type=jnp.float32
        )
        slot = jnp.sum(onehot * (count + carry), axis=0, keepdims=True)
        carry = carry + jnp.sum(onehot, axis=1, keepdims=True)
        targets.append(pick * SLOTS + slot.astype(jnp.int32))
        target_ref[k : k + 1, :] = targets[k]
    chunk = 256
    for at in range(0, rows_ref.shape[0], chunk):
        row = at + lax.broadcasted_iota(jnp.int32, (chunk, tokens), 0)
        chosen = jnp.concatenate(
            [jnp.where(row == target, 1.0, 0.0).astype(jnp.bfloat16) for target in targets], axis=1
        )
        rows_ref[at : at + chunk, :] = jnp.dot(
            chosen, hidden_ref[...], preferred_element_type=jnp.float32
        ).astype(jnp.bfloat16)


def route(picks, hidden, experts):
    return pl.pallas_call(
        functools.partial(route_kernel, experts=experts),
        out_shape=(
            jax.ShapeDtypeStruct((experts * SLOTS, hidden.shape[1]), jnp.bfloat16),
            jax.ShapeDtypeStruct((WIDE, picks.shape[1]), jnp.int32),
        ),
        compiler_params=pltpu.CompilerParams(vmem_limit_bytes=VMEM),
        name="route",
    )(picks, hidden)


def expert_kernel(head_ref, own_ref, other_ref, own_w_ref, other_w_ref, out_ref):
    sources, _, depth = own_ref.shape
    for e in range(own_w_ref.shape[0]):
        at = slice(e * SLOTS, (e + 1) * SLOTS)
        own = own_ref[:, at, :].reshape(sources * SLOTS, depth)
        other = other_ref[:, at, :].reshape(sources * SLOTS, depth)
        total = jnp.dot(own, own_w_ref[e, 0], preferred_element_type=jnp.float32)
        total = total + jnp.dot(other, other_w_ref[e, 0], preferred_element_type=jnp.float32)
        out_ref[:, at, :] = total.astype(jnp.bfloat16).reshape(sources, SLOTS, -1)


def run_experts(head, own, other, weight):
    sources, rows, depth = own.shape
    local, _, _, width = weight.shape
    step = 8
    return pl.pallas_call(
        expert_kernel,
        out_shape=jax.ShapeDtypeStruct((sources, rows, width), jnp.bfloat16),
        grid_spec=pltpu.PrefetchScalarGridSpec(
            num_scalar_prefetch=1,
            grid=(sources // step,),
            in_specs=[
                pl.BlockSpec((step, rows, depth), lambda i, h: (i, 0, 0)),
                pl.BlockSpec((step, rows, depth), lambda i, h: (i, 0, 0)),
                pl.BlockSpec((local, 1, depth, width), lambda i, h: (0, h[0], 0, 0)),
                pl.BlockSpec((local, 1, depth, width), lambda i, h: (0, 1 - h[0], 0, 0)),
            ],
            out_specs=pl.BlockSpec((step, rows, width), lambda i, h: (i, 0, 0)),
        ),
        compiler_params=pltpu.CompilerParams(vmem_limit_bytes=VMEM),
        name="experts",
    )(head, own, other, weight, weight)


def combine_kernel(target_ref, level_ref, back_ref, out_ref, high_ref, low_ref, wide_ref):
    tokens, rows = high_ref.shape
    chunk = 256

    @pl.when(pl.program_id(0) == 0)
    def _():
        top = level_ref.shape[0]
        wide_ref[...] = jnp.zeros_like(wide_ref)
        wide_ref[0:top, :] = level_ref[...].astype(jnp.float32)
        level = wide_ref[...].T
        target = target_ref[...].astype(jnp.float32).T.astype(jnp.int32)
        for at in range(0, rows, chunk):
            row = at + lax.broadcasted_iota(jnp.int32, (tokens, chunk), 1)
            gate = jnp.zeros((tokens, chunk), jnp.float32)
            for k in range(top):
                gate = jnp.where(row == target[:, k : k + 1], level[:, k : k + 1], gate)
            high = gate.astype(jnp.bfloat16)
            high_ref[:, at : at + chunk] = high
            low_ref[:, at : at + chunk] = (gate - high.astype(jnp.float32)).astype(jnp.bfloat16)

    back = back_ref[...]
    total = jnp.dot(high_ref[...], back, preferred_element_type=jnp.float32)
    total = total + jnp.dot(low_ref[...], back, preferred_element_type=jnp.float32)
    out_ref[...] = (total * (1.0 / 1024.0)).astype(jnp.bfloat16)


def combine(target, levels, back):
    tokens = levels.shape[1]
    rows, width = back.shape
    tile = 256
    return pl.pallas_call(
        combine_kernel,
        out_shape=jax.ShapeDtypeStruct((tokens, width), jnp.bfloat16),
        grid=(width // tile,),
        in_specs=[
            pl.BlockSpec(target.shape, lambda i: (0, 0)),
            pl.BlockSpec(levels.shape, lambda i: (0, 0)),
            pl.BlockSpec((rows, tile), lambda i: (0, i)),
        ],
        out_specs=pl.BlockSpec((tokens, tile), lambda i: (0, i)),
        scratch_shapes=[
            pltpu.VMEM((tokens, rows), jnp.bfloat16),
            pltpu.VMEM((tokens, rows), jnp.bfloat16),
            pltpu.VMEM((WIDE, tokens), jnp.float32),
        ],
        compiler_params=pltpu.CompilerParams(vmem_limit_bytes=VMEM),
        name="combine",
    )(target, levels, back)


def shards(hidden_acts, picks, levels, down_weight):
    tokens, top = picks.shape
    half = hidden_acts.shape[-1]
    local, _, width = down_weight.shape
    devices = lax.axis_size("exp")
    experts = local * devices
    flat_hidden = jnp.transpose(hidden_acts, (1, 0, 2)).reshape(top * tokens, half)
    rows, target = route(picks.T, flat_hidden, experts)
    own = lax.all_to_all(
        rows.reshape(devices, local * SLOTS, half), "exp", split_axis=0, concat_axis=0, tiled=True
    )
    other = lax.ppermute(own, "head", [(0, 1), (1, 0)])
    head = lax.axis_index("head").astype(jnp.int32).reshape(1)
    outputs = run_experts(head, own, other, down_weight.reshape(local, 2, half, width))
    back = lax.all_to_all(outputs, "exp", split_axis=0, concat_axis=0, tiled=True)
    return combine(target, levels.T, back.reshape(experts * SLOTS, width))


def solution(mesh):
    placed = (
        P(("req", "exp"), None, "head"),
        P(("req", "exp"), None),
        P(("req", "exp"), None),
        P("exp", None, "head"),
    )
    return jax.shard_map(
        shards, mesh=mesh, in_specs=placed, out_specs=P(("req", "exp"), "head"), check_vma=False
    )
```

```python
import functools

import jax
import jax.numpy as jnp
from jax import lax
from jax.experimental import pallas as pl
from jax.experimental.pallas import tpu as pltpu
from jax.sharding import PartitionSpec as P

WIDE = 8
SLOTS = 16
VMEM = 24 * 1024 * 1024
WHOLE = pl.BlockSpec(memory_space=pltpu.VMEM)


def route_kernel(pick_ref, hidden_ref, rows_ref, target_ref, *, experts):
    top, tokens = pick_ref.shape
    before = lax.broadcasted_iota(jnp.int32, (tokens, tokens), 0)
    after = lax.broadcasted_iota(jnp.int32, (tokens, tokens), 1)
    earlier = jnp.where(before < after, 1.0, 0.0).astype(jnp.bfloat16)
    named = lax.broadcasted_iota(jnp.int32, (experts, tokens), 0)
    carry = jnp.zeros((experts, 1), jnp.float32)
    target_ref[...] = jnp.full(target_ref.shape, -1, jnp.int32)
    targets = []
    for k in range(top):
        pick = pick_ref[k : k + 1, :]
        onehot = jnp.where(named == pick, 1.0, 0.0)
        count = jnp.dot(
            onehot.astype(jnp.bfloat16), earlier, preferred_element_type=jnp.float32
        )
        slot = jnp.sum(onehot * (count + carry), axis=0, keepdims=True)
        carry = carry + jnp.sum(onehot, axis=1, keepdims=True)
        targets.append(pick * SLOTS + slot.astype(jnp.int32))
        target_ref[k : k + 1, :] = targets[k]
    chunk = 256
    for at in range(0, rows_ref.shape[0], chunk):
        row = at + lax.broadcasted_iota(jnp.int32, (chunk, tokens), 0)
        chosen = jnp.concatenate(
            [jnp.where(row == target, 1.0, 0.0).astype(jnp.bfloat16) for target in targets], axis=1
        )
        rows_ref[at : at + chunk, :] = jnp.dot(
            chosen, hidden_ref[...], preferred_element_type=jnp.float32
        ).astype(jnp.bfloat16)


def route(picks, hidden, experts):
    return pl.pallas_call(
        functools.partial(route_kernel, experts=experts),
        out_shape=(
            jax.ShapeDtypeStruct((experts * SLOTS, hidden.shape[1]), jnp.bfloat16),
            jax.ShapeDtypeStruct((WIDE, picks.shape[1]), jnp.int32),
        ),
        compiler_params=pltpu.CompilerParams(vmem_limit_bytes=VMEM),
        name="route",
    )(picks, hidden)


def expert_kernel(head_ref, own_ref, other_ref, weight_ref, out_ref):
    sources, _, half = own_ref.shape
    local, _, width = weight_ref.shape
    first = head_ref[0] == 0
    tile = 256
    for e in range(local):
        at = slice(e * SLOTS, (e + 1) * SLOTS)
        own = own_ref[:, at, :].reshape(sources * SLOTS, half)
        other = other_ref[:, at, :].reshape(sources * SLOTS, half)
        whole = jnp.concatenate(
            [jnp.where(first, own, other), jnp.where(first, other, own)], axis=1
        )
        for n in range(0, width, tile):
            total = jnp.dot(
                whole, weight_ref[e, :, n : n + tile], preferred_element_type=jnp.float32
            )
            out_ref[:, at, n : n + tile] = total.astype(jnp.bfloat16).reshape(sources, SLOTS, tile)


def run_experts(head, own, other, weight):
    sources, rows, half = own.shape
    local, depth, width = weight.shape
    return pl.pallas_call(
        expert_kernel,
        out_shape=jax.ShapeDtypeStruct((sources, rows, width), jnp.bfloat16),
        in_specs=[pl.BlockSpec(memory_space=pltpu.SMEM), WHOLE, WHOLE, WHOLE],
        out_specs=WHOLE,
        compiler_params=pltpu.CompilerParams(vmem_limit_bytes=VMEM),
        cost_estimate=pl.CostEstimate(
            flops=2 * sources * rows * depth * width, bytes_accessed=12 << 20, transcendentals=0
        ),
        name="experts",
    )(head, own, other, weight)


def gates_kernel(target_ref, level_ref, gates_ref, wide_ref):
    tokens, rows = gates_ref.shape[1:]
    top = level_ref.shape[0]
    chunk = 256
    wide_ref[...] = jnp.zeros_like(wide_ref)
    wide_ref[0:top, :] = level_ref[...].astype(jnp.float32)
    level = wide_ref[...].T
    target = target_ref[...].astype(jnp.float32).T.astype(jnp.int32)
    for at in range(0, rows, chunk):
        row = at + lax.broadcasted_iota(jnp.int32, (tokens, chunk), 1)
        gate = jnp.zeros((tokens, chunk), jnp.float32)
        for k in range(top):
            gate = jnp.where(row == target[:, k : k + 1], level[:, k : k + 1], gate)
        high = gate.astype(jnp.bfloat16)
        gates_ref[0, :, at : at + chunk] = high
        gates_ref[1, :, at : at + chunk] = (gate - high.astype(jnp.float32)).astype(jnp.bfloat16)


def make_gates(target, levels, rows):
    tokens = levels.shape[1]
    return pl.pallas_call(
        gates_kernel,
        out_shape=jax.ShapeDtypeStruct((2, tokens, rows), jnp.bfloat16),
        in_specs=[WHOLE, WHOLE],
        out_specs=WHOLE,
        scratch_shapes=[pltpu.VMEM((WIDE, tokens), jnp.float32)],
        compiler_params=pltpu.CompilerParams(vmem_limit_bytes=VMEM),
        cost_estimate=pl.CostEstimate(flops=4 << 20, bytes_accessed=8 << 20, transcendentals=0),
        name="gates",
    )(target, levels)


def combine_kernel(gates_ref, back_ref, out_ref):
    tile = 256
    for n in range(0, out_ref.shape[1], tile):
        back = back_ref[:, n : n + tile]
        total = jnp.dot(gates_ref[0], back, preferred_element_type=jnp.float32)
        total = total + jnp.dot(gates_ref[1], back, preferred_element_type=jnp.float32)
        out_ref[:, n : n + tile] = (total * (1.0 / 1024.0)).astype(jnp.bfloat16)


def combine(gates, back):
    return pl.pallas_call(
        combine_kernel,
        out_shape=jax.ShapeDtypeStruct((gates.shape[1], back.shape[1]), jnp.bfloat16),
        in_specs=[WHOLE, WHOLE],
        out_specs=WHOLE,
        compiler_params=pltpu.CompilerParams(vmem_limit_bytes=VMEM),
        name="combine",
    )(gates, back)


def shards(hidden_acts, picks, levels, down_weight):
    tokens, top = picks.shape
    half = hidden_acts.shape[-1]
    local, _, width = down_weight.shape
    devices = lax.axis_size("exp")
    experts = local * devices
    flat_hidden = jnp.transpose(hidden_acts, (1, 0, 2)).reshape(top * tokens, half)
    rows, target = route(picks.T, flat_hidden, experts)
    own = lax.all_to_all(
        rows.reshape(devices, local * SLOTS, half), "exp", split_axis=0, concat_axis=0, tiled=True
    )
    other = lax.ppermute(own, "head", [(0, 1), (1, 0)])
    head = lax.axis_index("head").astype(jnp.int32).reshape(1)
    outputs = run_experts(head, own, other, down_weight)
    back = lax.all_to_all(outputs, "exp", split_axis=0, concat_axis=0, tiled=True)
    gates = make_gates(target, levels.T, experts * SLOTS)
    return combine(gates, back.reshape(experts * SLOTS, width))


def solution(mesh):
    placed = (
        P(("req", "exp"), None, "head"),
        P(("req", "exp"), None),
        P(("req", "exp"), None),
        P("exp", None, "head"),
    )
    return jax.shard_map(
        shards, mesh=mesh, in_specs=placed, out_specs=P(("req", "exp"), "head"), check_vma=False
    )
```

```python
import functools

import jax
import jax.numpy as jnp
from jax import lax
from jax.experimental import pallas as pl
from jax.experimental.pallas import tpu as pltpu
from jax.sharding import PartitionSpec as P

WIDE = 8
SLOTS = 16
VMEM = 24 * 1024 * 1024
WHOLE = pl.BlockSpec(memory_space=pltpu.VMEM)
FAR = pl.BlockSpec(memory_space=pltpu.HBM)


def route_kernel(pick_ref, hidden_ref, rows_ref, target_ref, *, experts):
    top, tokens = pick_ref.shape
    before = lax.broadcasted_iota(jnp.int32, (tokens, tokens), 0)
    after = lax.broadcasted_iota(jnp.int32, (tokens, tokens), 1)
    earlier = jnp.where(before < after, 1.0, 0.0).astype(jnp.bfloat16)
    named = lax.broadcasted_iota(jnp.int32, (experts, tokens), 0)
    carry = jnp.zeros((experts, 1), jnp.float32)
    target_ref[...] = jnp.full(target_ref.shape, -1, jnp.int32)
    targets = []
    for k in range(top):
        pick = pick_ref[k : k + 1, :]
        onehot = jnp.where(named == pick, 1.0, 0.0)
        count = jnp.dot(
            onehot.astype(jnp.bfloat16), earlier, preferred_element_type=jnp.float32
        )
        slot = jnp.sum(onehot * (count + carry), axis=0, keepdims=True)
        carry = carry + jnp.sum(onehot, axis=1, keepdims=True)
        targets.append(pick * SLOTS + slot.astype(jnp.int32))
        target_ref[k : k + 1, :] = targets[k]
    chunk = 256
    for at in range(0, rows_ref.shape[0], chunk):
        row = at + lax.broadcasted_iota(jnp.int32, (chunk, tokens), 0)
        chosen = jnp.concatenate(
            [jnp.where(row == target, 1.0, 0.0).astype(jnp.bfloat16) for target in targets], axis=1
        )
        rows_ref[at : at + chunk, :] = jnp.dot(
            chosen, hidden_ref[...], preferred_element_type=jnp.float32
        ).astype(jnp.bfloat16)


def route(picks, hidden, experts):
    return pl.pallas_call(
        functools.partial(route_kernel, experts=experts),
        out_shape=(
            jax.ShapeDtypeStruct((experts * SLOTS, hidden.shape[1]), jnp.bfloat16),
            jax.ShapeDtypeStruct((WIDE, picks.shape[1]), jnp.int32),
        ),
        in_specs=[WHOLE, WHOLE],
        out_specs=(WHOLE, WHOLE),
        compiler_params=pltpu.CompilerParams(vmem_limit_bytes=VMEM),
        name="route",
    )(picks, hidden)


def expert_kernel(head_ref, own_ref, other_ref, weight_ref, out_ref):
    sources, _, half = own_ref.shape
    local, _, width = weight_ref.shape
    first = head_ref[0] == 0
    tile = 256
    for e in range(local):
        at = slice(e * SLOTS, (e + 1) * SLOTS)
        own = own_ref[:, at, :].reshape(sources * SLOTS, half)
        other = other_ref[:, at, :].reshape(sources * SLOTS, half)
        whole = jnp.concatenate(
            [jnp.where(first, own, other), jnp.where(first, other, own)], axis=1
        )
        for n in range(0, width, tile):
            total = jnp.dot(
                whole, weight_ref[e, :, n : n + tile], preferred_element_type=jnp.float32
            )
            out_ref[:, at, n : n + tile] = total.astype(jnp.bfloat16).reshape(sources, SLOTS, tile)


def run_experts(head, own, other, weight):
    sources, rows, half = own.shape
    local, depth, width = weight.shape
    return pl.pallas_call(
        expert_kernel,
        out_shape=jax.ShapeDtypeStruct((sources, rows, width), jnp.bfloat16),
        in_specs=[pl.BlockSpec(memory_space=pltpu.SMEM), WHOLE, WHOLE, WHOLE],
        out_specs=WHOLE,
        compiler_params=pltpu.CompilerParams(vmem_limit_bytes=VMEM),
        cost_estimate=pl.CostEstimate(
            flops=2 * sources * rows * depth * width, bytes_accessed=12 << 20, transcendentals=0
        ),
        name="experts",
    )(head, own, other, weight)


def prepare_kernel(target_ref, level_ref, weight_hbm, gates_ref, weight_ref, wide_ref, sem):
    copy = pltpu.make_async_copy(weight_hbm, weight_ref, sem)
    copy.start()
    tokens, rows = gates_ref.shape[1:]
    top = level_ref.shape[0]
    chunk = 256
    wide_ref[...] = jnp.zeros_like(wide_ref)
    wide_ref[0:top, :] = level_ref[...].astype(jnp.float32)
    level = wide_ref[...].T
    target = target_ref[...].astype(jnp.float32).T.astype(jnp.int32)
    for at in range(0, rows, chunk):
        row = at + lax.broadcasted_iota(jnp.int32, (tokens, chunk), 1)
        gate = jnp.zeros((tokens, chunk), jnp.float32)
        for k in range(top):
            gate = jnp.where(row == target[:, k : k + 1], level[:, k : k + 1], gate)
        high = gate.astype(jnp.bfloat16)
        gates_ref[0, :, at : at + chunk] = high
        gates_ref[1, :, at : at + chunk] = (gate - high.astype(jnp.float32)).astype(jnp.bfloat16)
    copy.wait()


def prepare(target, levels, weight, rows):
    tokens = levels.shape[1]
    return pl.pallas_call(
        prepare_kernel,
        out_shape=(
            jax.ShapeDtypeStruct((2, tokens, rows), jnp.bfloat16),
            jax.ShapeDtypeStruct(weight.shape, jnp.bfloat16),
        ),
        in_specs=[WHOLE, WHOLE, FAR],
        out_specs=(WHOLE, WHOLE),
        scratch_shapes=[pltpu.VMEM((WIDE, tokens), jnp.float32), pltpu.SemaphoreType.DMA],
        compiler_params=pltpu.CompilerParams(vmem_limit_bytes=VMEM),
        cost_estimate=pl.CostEstimate(flops=4 << 20, bytes_accessed=8 << 20, transcendentals=0),
        name="prepare",
    )(target, levels, weight)


def combine_kernel(gates_ref, back_ref, out_ref):
    tile = 256
    for n in range(0, out_ref.shape[1], tile):
        back = back_ref[:, n : n + tile]
        total = jnp.dot(gates_ref[0], back, preferred_element_type=jnp.float32)
        total = total + jnp.dot(gates_ref[1], back, preferred_element_type=jnp.float32)
        out_ref[:, n : n + tile] = (total * (1.0 / 1024.0)).astype(jnp.bfloat16)


def combine(gates, back):
    return pl.pallas_call(
        combine_kernel,
        out_shape=jax.ShapeDtypeStruct((gates.shape[1], back.shape[1]), jnp.bfloat16),
        in_specs=[WHOLE, WHOLE],
        out_specs=WHOLE,
        compiler_params=pltpu.CompilerParams(vmem_limit_bytes=VMEM),
        name="combine",
    )(gates, back)


def shards(hidden_acts, picks, levels, down_weight):
    tokens, top = picks.shape
    half = hidden_acts.shape[-1]
    local, _, width = down_weight.shape
    devices = lax.axis_size("exp")
    experts = local * devices
    flat_hidden = jnp.transpose(hidden_acts, (1, 0, 2)).reshape(top * tokens, half)
    rows, target = route(picks.T, flat_hidden, experts)
    own = lax.all_to_all(
        rows.reshape(devices, local * SLOTS, half), "exp", split_axis=0, concat_axis=0, tiled=True
    )
    other = lax.ppermute(own, "head", [(0, 1), (1, 0)])
    head = lax.axis_index("head").astype(jnp.int32).reshape(1)
    gates, weight = prepare(target, levels.T, down_weight, experts * SLOTS)
    other, gates, weight = lax.optimization_barrier((other, gates, weight))
    outputs = run_experts(head, own, other, weight)
    back = lax.all_to_all(outputs, "exp", split_axis=0, concat_axis=0, tiled=True)
    return combine(gates, back.reshape(experts * SLOTS, width))


def solution(mesh):
    placed = (
        P(("req", "exp"), None, "head"),
        P(("req", "exp"), None),
        P(("req", "exp"), None),
        P("exp", None, "head"),
    )
    return jax.shard_map(
        shards, mesh=mesh, in_specs=placed, out_specs=P(("req", "exp"), "head"), check_vma=False
    )
```

```python
import functools

import jax
import jax.numpy as jnp
from jax import lax
from jax.experimental import pallas as pl
from jax.experimental.pallas import tpu as pltpu
from jax.sharding import PartitionSpec as P

WIDE = 8
SLOTS = 16
VMEM = 24 * 1024 * 1024
WHOLE = pl.BlockSpec(memory_space=pltpu.VMEM)
FAR = pl.BlockSpec(memory_space=pltpu.HBM)


def far(array):
    return pltpu.with_memory_space_constraint(array, pltpu.HBM)


def route_kernel(
    picks_far, hidden_far, rows_ref, target_ref, pick_ref, hidden_ref, pick_sem, hidden_sem, *, experts
):
    pick_copy = pltpu.make_async_copy(picks_far, pick_ref, pick_sem)
    hidden_copy = pltpu.make_async_copy(hidden_far, hidden_ref, hidden_sem)
    pick_copy.start()
    hidden_copy.start()
    pick_copy.wait()
    top, tokens = pick_ref.shape
    before = lax.broadcasted_iota(jnp.int32, (tokens, tokens), 0)
    after = lax.broadcasted_iota(jnp.int32, (tokens, tokens), 1)
    earlier = jnp.where(before < after, 1.0, 0.0).astype(jnp.bfloat16)
    named = lax.broadcasted_iota(jnp.int32, (experts, tokens), 0)
    carry = jnp.zeros((experts, 1), jnp.float32)
    target_ref[...] = jnp.full(target_ref.shape, -1, jnp.int32)
    targets = []
    for k in range(top):
        pick = pick_ref[k : k + 1, :]
        onehot = jnp.where(named == pick, 1.0, 0.0)
        count = jnp.dot(
            onehot.astype(jnp.bfloat16), earlier, preferred_element_type=jnp.float32
        )
        slot = jnp.sum(onehot * (count + carry), axis=0, keepdims=True)
        carry = carry + jnp.sum(onehot, axis=1, keepdims=True)
        targets.append(pick * SLOTS + slot.astype(jnp.int32))
        target_ref[k : k + 1, :] = targets[k]
    hidden_copy.wait()
    chunk = 256
    for at in range(0, rows_ref.shape[0], chunk):
        row = at + lax.broadcasted_iota(jnp.int32, (chunk, tokens), 0)
        chosen = jnp.concatenate(
            [jnp.where(row == target, 1.0, 0.0).astype(jnp.bfloat16) for target in targets], axis=1
        )
        rows_ref[at : at + chunk, :] = jnp.dot(
            chosen, hidden_ref[...], preferred_element_type=jnp.float32
        ).astype(jnp.bfloat16)


def route(picks, hidden, experts):
    return pl.pallas_call(
        functools.partial(route_kernel, experts=experts),
        out_shape=(
            jax.ShapeDtypeStruct((experts * SLOTS, hidden.shape[1]), jnp.bfloat16),
            jax.ShapeDtypeStruct((WIDE, picks.shape[1]), jnp.int32),
        ),
        in_specs=[FAR, FAR],
        out_specs=(WHOLE, WHOLE),
        scratch_shapes=[
            pltpu.VMEM(picks.shape, jnp.int32),
            pltpu.VMEM(hidden.shape, jnp.bfloat16),
            pltpu.SemaphoreType.DMA,
            pltpu.SemaphoreType.DMA,
        ],
        compiler_params=pltpu.CompilerParams(vmem_limit_bytes=VMEM),
        name="route",
    )(far(picks), far(hidden))


def expert_kernel(head_ref, own_ref, other_ref, weight_ref, out_ref):
    sources, _, half = own_ref.shape
    local, _, width = weight_ref.shape
    first = head_ref[0] == 0
    tile = 256
    for e in range(local):
        at = slice(e * SLOTS, (e + 1) * SLOTS)
        own = own_ref[:, at, :].reshape(sources * SLOTS, half)
        other = other_ref[:, at, :].reshape(sources * SLOTS, half)
        whole = jnp.concatenate(
            [jnp.where(first, own, other), jnp.where(first, other, own)], axis=1
        )
        for n in range(0, width, tile):
            total = jnp.dot(
                whole, weight_ref[e, :, n : n + tile], preferred_element_type=jnp.float32
            )
            out_ref[:, at, n : n + tile] = total.astype(jnp.bfloat16).reshape(sources, SLOTS, tile)


def run_experts(head, own, other, weight):
    sources, rows, half = own.shape
    local, depth, width = weight.shape
    return pl.pallas_call(
        expert_kernel,
        out_shape=jax.ShapeDtypeStruct((sources, rows, width), jnp.bfloat16),
        in_specs=[pl.BlockSpec(memory_space=pltpu.SMEM), WHOLE, WHOLE, WHOLE],
        out_specs=WHOLE,
        compiler_params=pltpu.CompilerParams(vmem_limit_bytes=VMEM),
        cost_estimate=pl.CostEstimate(
            flops=2 * sources * rows * depth * width, bytes_accessed=12 << 20, transcendentals=0
        ),
        name="experts",
    )(head, own, other, weight)


def prepare_kernel(target_ref, level_ref, weight_hbm, gates_ref, weight_ref, wide_ref, sem):
    copy = pltpu.make_async_copy(weight_hbm, weight_ref, sem)
    copy.start()
    tokens, rows = gates_ref.shape[1:]
    top = level_ref.shape[0]
    chunk = 256
    wide_ref[...] = jnp.zeros_like(wide_ref)
    wide_ref[0:top, :] = level_ref[...].astype(jnp.float32)
    level = wide_ref[...].T
    target = target_ref[...].astype(jnp.float32).T.astype(jnp.int32)
    for at in range(0, rows, chunk):
        row = at + lax.broadcasted_iota(jnp.int32, (tokens, chunk), 1)
        gate = jnp.zeros((tokens, chunk), jnp.float32)
        for k in range(top):
            gate = jnp.where(row == target[:, k : k + 1], level[:, k : k + 1], gate)
        high = gate.astype(jnp.bfloat16)
        gates_ref[0, :, at : at + chunk] = high
        gates_ref[1, :, at : at + chunk] = (gate - high.astype(jnp.float32)).astype(jnp.bfloat16)
    copy.wait()


def prepare(target, levels, weight, rows):
    tokens = levels.shape[1]
    return pl.pallas_call(
        prepare_kernel,
        out_shape=(
            jax.ShapeDtypeStruct((2, tokens, rows), jnp.bfloat16),
            jax.ShapeDtypeStruct(weight.shape, jnp.bfloat16),
        ),
        in_specs=[WHOLE, WHOLE, FAR],
        out_specs=(WHOLE, WHOLE),
        scratch_shapes=[pltpu.VMEM((WIDE, tokens), jnp.float32), pltpu.SemaphoreType.DMA],
        compiler_params=pltpu.CompilerParams(vmem_limit_bytes=VMEM),
        cost_estimate=pl.CostEstimate(flops=4 << 20, bytes_accessed=8 << 20, transcendentals=0),
        name="prepare",
    )(target, levels, far(weight))


def combine_kernel(gates_ref, back_ref, out_ref):
    tile = 256
    for n in range(0, out_ref.shape[1], tile):
        back = back_ref[:, n : n + tile]
        total = jnp.dot(gates_ref[0], back, preferred_element_type=jnp.float32)
        total = total + jnp.dot(gates_ref[1], back, preferred_element_type=jnp.float32)
        out_ref[:, n : n + tile] = (total * (1.0 / 1024.0)).astype(jnp.bfloat16)


def combine(gates, back):
    return pl.pallas_call(
        combine_kernel,
        out_shape=jax.ShapeDtypeStruct((gates.shape[1], back.shape[1]), jnp.bfloat16),
        in_specs=[WHOLE, WHOLE],
        out_specs=WHOLE,
        compiler_params=pltpu.CompilerParams(vmem_limit_bytes=VMEM),
        name="combine",
    )(gates, back)


def shards(hidden_acts, picks, levels, down_weight):
    tokens, top = picks.shape
    half = hidden_acts.shape[-1]
    local, _, width = down_weight.shape
    devices = lax.axis_size("exp")
    experts = local * devices
    flat_hidden = jnp.transpose(hidden_acts, (1, 0, 2)).reshape(top * tokens, half)
    rows, target = route(picks.T, flat_hidden, experts)
    own = lax.all_to_all(
        rows.reshape(devices, local * SLOTS, half), "exp", split_axis=0, concat_axis=0, tiled=True
    )
    other = lax.ppermute(own, "head", [(0, 1), (1, 0)])
    head = lax.axis_index("head").astype(jnp.int32).reshape(1)
    gates, weight = prepare(target, levels.T, down_weight, experts * SLOTS)
    other, gates, weight = lax.optimization_barrier((other, gates, weight))
    outputs = run_experts(head, own, other, weight)
    back = lax.all_to_all(outputs, "exp", split_axis=0, concat_axis=0, tiled=True)
    return combine(gates, back.reshape(experts * SLOTS, width))


def solution(mesh):
    placed = (
        P(("req", "exp"), None, "head"),
        P(("req", "exp"), None),
        P(("req", "exp"), None),
        P("exp", None, "head"),
    )
    return jax.shard_map(
        shards, mesh=mesh, in_specs=placed, out_specs=P(("req", "exp"), "head"), check_vma=False
    )
```

```python
import functools

import jax
import jax.numpy as jnp
from jax import lax
from jax.experimental import pallas as pl
from jax.experimental.pallas import tpu as pltpu
from jax.sharding import PartitionSpec as P

LANES = 128
WIDE = 8
SLOTS = 16
VMEM = 24 * 1024 * 1024
WHOLE = pl.BlockSpec(memory_space=pltpu.VMEM)
FAR = pl.BlockSpec(memory_space=pltpu.HBM)


def far(array):
    return pltpu.with_memory_space_constraint(array, pltpu.HBM)


def route_kernel(
    picks_far, hidden_far, rows_ref, target_ref, pick_ref, hidden_ref, pick_sem, hidden_sem, *, experts
):
    pick_copy = pltpu.make_async_copy(picks_far, pick_ref, pick_sem)
    hidden_copy = pltpu.make_async_copy(hidden_far, hidden_ref, hidden_sem)
    pick_copy.start()
    hidden_copy.start()
    pick_copy.wait()
    top, tokens = pick_ref.shape
    before = lax.broadcasted_iota(jnp.int32, (tokens, tokens), 0)
    after = lax.broadcasted_iota(jnp.int32, (tokens, tokens), 1)
    earlier = jnp.where(before < after, 1.0, 0.0).astype(jnp.bfloat16)
    named = lax.broadcasted_iota(jnp.int32, (experts, tokens), 0)
    carry = jnp.zeros((experts, 1), jnp.float32)
    target_ref[...] = jnp.full(target_ref.shape, -1, jnp.int32)
    targets = []
    for k in range(top):
        pick = pick_ref[k : k + 1, :]
        onehot = jnp.where(named == pick, 1.0, 0.0)
        count = jnp.dot(
            onehot.astype(jnp.bfloat16), earlier, preferred_element_type=jnp.float32
        )
        slot = jnp.sum(onehot * (count + carry), axis=0, keepdims=True)
        carry = carry + jnp.sum(onehot, axis=1, keepdims=True)
        targets.append(pick * SLOTS + slot.astype(jnp.int32))
        target_ref[k : k + 1, :] = targets[k]
    hidden_copy.wait()
    chunk = 256
    for at in range(0, rows_ref.shape[0], chunk):
        row = at + lax.broadcasted_iota(jnp.int32, (chunk, tokens), 0)
        chosen = jnp.concatenate(
            [jnp.where(row == target, 1.0, 0.0).astype(jnp.bfloat16) for target in targets], axis=1
        )
        rows_ref[at : at + chunk, :] = jnp.dot(
            chosen, hidden_ref[...], preferred_element_type=jnp.float32
        ).astype(jnp.bfloat16)


def route(picks, hidden, experts):
    return pl.pallas_call(
        functools.partial(route_kernel, experts=experts),
        out_shape=(
            jax.ShapeDtypeStruct((experts * SLOTS, hidden.shape[1]), jnp.bfloat16),
            jax.ShapeDtypeStruct((WIDE, picks.shape[1]), jnp.int32),
        ),
        in_specs=[FAR, FAR],
        out_specs=(WHOLE, WHOLE),
        scratch_shapes=[
            pltpu.VMEM(picks.shape, jnp.int32),
            pltpu.VMEM(hidden.shape, jnp.bfloat16),
            pltpu.SemaphoreType.DMA,
            pltpu.SemaphoreType.DMA,
        ],
        compiler_params=pltpu.CompilerParams(vmem_limit_bytes=VMEM),
        name="route",
    )(far(picks), far(hidden))


def expert_kernel(head_ref, own_ref, other_ref, weight_ref, out_ref):
    sources, _, half = own_ref.shape
    width = weight_ref.shape[2]
    first = head_ref[0] == 0
    last_row = lax.broadcasted_iota(jnp.int32, (sources, SLOTS, LANES), 1) == SLOTS - 1
    tile = 2 * LANES
    parts = width // tile

    def halves(e):
        at = slice(e * SLOTS, (e + 1) * SLOTS)
        own = own_ref[:, at, :].reshape(sources * SLOTS, half)
        other = other_ref[:, at, :].reshape(sources * SLOTS, half)
        return jnp.concatenate(
            [jnp.where(first, own, other), jnp.where(first, other, own)], axis=1
        )

    def product(whole, e, n):
        total = jnp.dot(
            whole, weight_ref[e, :, n * tile : (n + 1) * tile], preferred_element_type=jnp.float32
        )
        return [total[:, i * LANES : (i + 1) * LANES].reshape(sources, SLOTS, LANES) for i in (0, 1)]

    def put(j, block):
        if j < SLOTS - 1:
            block = jnp.where(last_row, folded[:, j : j + 1, :], block)
        out_ref[:, :, j * LANES : (j + 1) * LANES] = block.astype(jnp.bfloat16)

    whole = halves(1)
    left, folded = product(whole, 1, parts - 1)
    put(4 * parts - 2, left)
    for n in range(parts - 1):
        for i, block in enumerate(product(whole, 1, n)):
            put(2 * (parts + n) + i, block)
    whole = halves(0)
    for n in range(parts):
        for i, block in enumerate(product(whole, 0, n)):
            put(2 * n + i, block)


def run_experts(head, own, other, weight):
    sources, rows, half = own.shape
    local, depth, width = weight.shape
    assert local == 2 and width % (2 * LANES) == 0 and 2 * width >= SLOTS * LANES
    return pl.pallas_call(
        expert_kernel,
        out_shape=jax.ShapeDtypeStruct((sources, SLOTS, 2 * width - LANES), jnp.bfloat16),
        in_specs=[pl.BlockSpec(memory_space=pltpu.SMEM), WHOLE, WHOLE, WHOLE],
        out_specs=WHOLE,
        compiler_params=pltpu.CompilerParams(vmem_limit_bytes=VMEM),
        cost_estimate=pl.CostEstimate(
            flops=2 * sources * rows * depth * width, bytes_accessed=12 << 20, transcendentals=0
        ),
        name="experts",
    )(head, own, other, weight)


def prepare_kernel(target_ref, level_ref, weight_hbm, gates_ref, weight_ref, wide_ref, sem):
    copy = pltpu.make_async_copy(weight_hbm, weight_ref, sem)
    copy.start()
    tokens, rows = gates_ref.shape[1:]
    top = level_ref.shape[0]
    chunk = 256
    wide_ref[...] = jnp.zeros_like(wide_ref)
    wide_ref[0:top, :] = level_ref[...].astype(jnp.float32)
    level = wide_ref[...].T
    row_of = target_ref[...]
    row_of = (
        ((row_of // SLOTS) % 2) * (rows // 2) + (row_of // (2 * SLOTS)) * SLOTS + row_of % SLOTS
    )
    target = row_of.astype(jnp.float32).T.astype(jnp.int32)
    for at in range(0, rows, chunk):
        row = at + lax.broadcasted_iota(jnp.int32, (tokens, chunk), 1)
        gate = jnp.zeros((tokens, chunk), jnp.float32)
        for k in range(top):
            gate = jnp.where(row == target[:, k : k + 1], level[:, k : k + 1], gate)
        high = gate.astype(jnp.bfloat16)
        gates_ref[0, :, at : at + chunk] = high
        gates_ref[1, :, at : at + chunk] = (gate - high.astype(jnp.float32)).astype(jnp.bfloat16)
    copy.wait()


def prepare(target, levels, weight, rows):
    tokens = levels.shape[1]
    return pl.pallas_call(
        prepare_kernel,
        out_shape=(
            jax.ShapeDtypeStruct((2, tokens, rows), jnp.bfloat16),
            jax.ShapeDtypeStruct(weight.shape, jnp.bfloat16),
        ),
        in_specs=[WHOLE, WHOLE, FAR],
        out_specs=(WHOLE, WHOLE),
        scratch_shapes=[pltpu.VMEM((WIDE, tokens), jnp.float32), pltpu.SemaphoreType.DMA],
        compiler_params=pltpu.CompilerParams(vmem_limit_bytes=VMEM),
        cost_estimate=pl.CostEstimate(flops=4 << 20, bytes_accessed=8 << 20, transcendentals=0),
        name="prepare",
    )(target, levels, far(weight))


def combine_kernel(gates_ref, back_ref, out_ref):
    sources, _, lanes = back_ref.shape
    width = out_ref.shape[1]
    rows = sources * SLOTS
    tile = 2 * LANES
    row = lax.broadcasted_iota(jnp.int32, (sources, SLOTS, LANES), 1)
    unfolded = jnp.zeros((sources, SLOTS, LANES), jnp.float32)
    for j in range(SLOTS - 1):
        block = back_ref[:, :, j * LANES : (j + 1) * LANES].astype(jnp.float32)
        unfolded = jnp.where(row == j, block[:, SLOTS - 1 : SLOTS, :], unfolded)
    unfolded = unfolded.astype(jnp.bfloat16).reshape(rows, LANES)

    def gated(e, back):
        at = slice(e * rows, (e + 1) * rows)
        high = jnp.dot(gates_ref[0, :, at], back, preferred_element_type=jnp.float32)
        return high + jnp.dot(gates_ref[1, :, at], back, preferred_element_type=jnp.float32)

    for n in range(0, width, tile):
        first = back_ref[:, :, n : n + tile].reshape(rows, tile)
        at = width + n
        if at + tile <= lanes:
            second = back_ref[:, :, at : at + tile].reshape(rows, tile)
        else:
            second = jnp.concatenate(
                [back_ref[:, :, at : at + LANES].reshape(rows, LANES), unfolded], axis=1
            )
        total = gated(0, first) + gated(1, second)
        out_ref[:, n : n + tile] = (total * (1.0 / 1024.0)).astype(jnp.bfloat16)


def combine(gates, back):
    return pl.pallas_call(
        combine_kernel,
        out_shape=jax.ShapeDtypeStruct(
            (gates.shape[1], (back.shape[2] + LANES) // 2), jnp.bfloat16
        ),
        in_specs=[WHOLE, WHOLE],
        out_specs=WHOLE,
        compiler_params=pltpu.CompilerParams(vmem_limit_bytes=VMEM),
        name="combine",
    )(gates, back)


def shards(hidden_acts, picks, levels, down_weight):
    tokens, top = picks.shape
    half = hidden_acts.shape[-1]
    local, _, width = down_weight.shape
    devices = lax.axis_size("exp")
    experts = local * devices
    flat_hidden = jnp.transpose(hidden_acts, (1, 0, 2)).reshape(top * tokens, half)
    rows, target = route(picks.T, flat_hidden, experts)
    own = lax.all_to_all(
        rows.reshape(devices, local * SLOTS, half), "exp", split_axis=0, concat_axis=0, tiled=True
    )
    other = lax.ppermute(own, "head", [(0, 1), (1, 0)])
    head = lax.axis_index("head").astype(jnp.int32).reshape(1)
    gates, weight = prepare(target, levels.T, down_weight, experts * SLOTS)
    other, gates, weight = lax.optimization_barrier((other, gates, weight))
    outputs = run_experts(head, own, other, weight)
    back = lax.all_to_all(outputs, "exp", split_axis=0, concat_axis=0, tiled=True)
    return combine(gates, back)


def solution(mesh):
    placed = (
        P(("req", "exp"), None, "head"),
        P(("req", "exp"), None),
        P(("req", "exp"), None),
        P("exp", None, "head"),
    )
    return jax.shard_map(
        shards, mesh=mesh, in_specs=placed, out_specs=P(("req", "exp"), "head"), check_vma=False
    )
```

```python
import functools

import jax
import jax.numpy as jnp
from jax import lax
from jax.experimental import pallas as pl
from jax.experimental.pallas import tpu as pltpu
from jax.sharding import PartitionSpec as P

LANES = 128
RING = 8
STRIDE = 3
WIDE = 8
SLOTS = 16
VMEM = 24 * 1024 * 1024
WHOLE = pl.BlockSpec(memory_space=pltpu.VMEM)
FAR = pl.BlockSpec(memory_space=pltpu.HBM)


def placed(expert):
    device, own = expert // 2, expert % 2
    return (device // RING * RING + device * STRIDE % RING) * 2 + own


def exchange(array):
    order = [z + y * STRIDE % RING for z in range(0, array.shape[0], RING) for y in range(RING)]
    return lax.all_to_all(
        array, "exp", split_axis=0, concat_axis=0, tiled=True, axis_index_groups=[order]
    )


def far(array):
    return pltpu.with_memory_space_constraint(array, pltpu.HBM)


def route_kernel(
    picks_far, hidden_far, rows_ref, target_ref, pick_ref, hidden_ref, pick_sem, hidden_sem, *, experts
):
    pick_copy = pltpu.make_async_copy(picks_far, pick_ref, pick_sem)
    hidden_copy = pltpu.make_async_copy(hidden_far, hidden_ref, hidden_sem)
    pick_copy.start()
    hidden_copy.start()
    pick_copy.wait()
    top, tokens = pick_ref.shape
    before = lax.broadcasted_iota(jnp.int32, (tokens, tokens), 0)
    after = lax.broadcasted_iota(jnp.int32, (tokens, tokens), 1)
    earlier = jnp.where(before < after, 1.0, 0.0).astype(jnp.bfloat16)
    named = lax.broadcasted_iota(jnp.int32, (experts, tokens), 0)
    carry = jnp.zeros((experts, 1), jnp.float32)
    target_ref[...] = jnp.full(target_ref.shape, -1, jnp.int32)
    targets = []
    for k in range(top):
        pick = pick_ref[k : k + 1, :]
        onehot = jnp.where(named == pick, 1.0, 0.0)
        count = jnp.dot(
            onehot.astype(jnp.bfloat16), earlier, preferred_element_type=jnp.float32
        )
        slot = jnp.sum(onehot * (count + carry), axis=0, keepdims=True)
        carry = carry + jnp.sum(onehot, axis=1, keepdims=True)
        targets.append(placed(pick) * SLOTS + slot.astype(jnp.int32))
        target_ref[k : k + 1, :] = targets[k]
    hidden_copy.wait()
    chunk = 256
    for at in range(0, rows_ref.shape[0], chunk):
        row = at + lax.broadcasted_iota(jnp.int32, (chunk, tokens), 0)
        chosen = jnp.concatenate(
            [jnp.where(row == target, 1.0, 0.0).astype(jnp.bfloat16) for target in targets], axis=1
        )
        rows_ref[at : at + chunk, :] = jnp.dot(
            chosen, hidden_ref[...], preferred_element_type=jnp.float32
        ).astype(jnp.bfloat16)


def route(picks, hidden, experts):
    return pl.pallas_call(
        functools.partial(route_kernel, experts=experts),
        out_shape=(
            jax.ShapeDtypeStruct((experts * SLOTS, hidden.shape[1]), jnp.bfloat16),
            jax.ShapeDtypeStruct((WIDE, picks.shape[1]), jnp.int32),
        ),
        in_specs=[FAR, FAR],
        out_specs=(WHOLE, WHOLE),
        scratch_shapes=[
            pltpu.VMEM(picks.shape, jnp.int32),
            pltpu.VMEM(hidden.shape, jnp.bfloat16),
            pltpu.SemaphoreType.DMA,
            pltpu.SemaphoreType.DMA,
        ],
        compiler_params=pltpu.CompilerParams(vmem_limit_bytes=VMEM),
        name="route",
    )(far(picks), far(hidden))


def expert_kernel(head_ref, own_ref, other_ref, weight_ref, out_ref):
    sources, _, half = own_ref.shape
    width = weight_ref.shape[2]
    first = head_ref[0] == 0
    last_row = lax.broadcasted_iota(jnp.int32, (sources, SLOTS, LANES), 1) == SLOTS - 1
    tile = 2 * LANES
    parts = width // tile

    def halves(e):
        at = slice(e * SLOTS, (e + 1) * SLOTS)
        own = own_ref[:, at, :].reshape(sources * SLOTS, half)
        other = other_ref[:, at, :].reshape(sources * SLOTS, half)
        return jnp.concatenate(
            [jnp.where(first, own, other), jnp.where(first, other, own)], axis=1
        )

    def product(whole, e, n):
        total = jnp.dot(
            whole, weight_ref[e, :, n * tile : (n + 1) * tile], preferred_element_type=jnp.float32
        )
        return [total[:, i * LANES : (i + 1) * LANES].reshape(sources, SLOTS, LANES) for i in (0, 1)]

    def put(j, block):
        if j < SLOTS - 1:
            block = jnp.where(last_row, folded[:, j : j + 1, :], block)
        out_ref[:, :, j * LANES : (j + 1) * LANES] = block.astype(jnp.bfloat16)

    whole = halves(1)
    left, folded = product(whole, 1, parts - 1)
    put(4 * parts - 2, left)
    for n in range(parts - 1):
        for i, block in enumerate(product(whole, 1, n)):
            put(2 * (parts + n) + i, block)
    whole = halves(0)
    for n in range(parts):
        for i, block in enumerate(product(whole, 0, n)):
            put(2 * n + i, block)


def run_experts(head, own, other, weight):
    sources, rows, half = own.shape
    local, depth, width = weight.shape
    assert local == 2 and width % (2 * LANES) == 0 and 2 * width >= SLOTS * LANES
    return pl.pallas_call(
        expert_kernel,
        out_shape=jax.ShapeDtypeStruct((sources, SLOTS, 2 * width - LANES), jnp.bfloat16),
        in_specs=[pl.BlockSpec(memory_space=pltpu.SMEM), WHOLE, WHOLE, WHOLE],
        out_specs=WHOLE,
        compiler_params=pltpu.CompilerParams(vmem_limit_bytes=VMEM),
        cost_estimate=pl.CostEstimate(
            flops=2 * sources * rows * depth * width, bytes_accessed=12 << 20, transcendentals=0
        ),
        name="experts",
    )(head, own, other, weight)


def prepare_kernel(target_ref, level_ref, weight_hbm, gates_ref, weight_ref, wide_ref, sem):
    copy = pltpu.make_async_copy(weight_hbm, weight_ref, sem)
    copy.start()
    tokens, rows = gates_ref.shape[1:]
    top = level_ref.shape[0]
    chunk = 256
    wide_ref[...] = jnp.zeros_like(wide_ref)
    wide_ref[0:top, :] = level_ref[...].astype(jnp.float32)
    level = wide_ref[...].T
    row_of = target_ref[...]
    row_of = (
        ((row_of // SLOTS) % 2) * (rows // 2) + (row_of // (2 * SLOTS)) * SLOTS + row_of % SLOTS
    )
    target = row_of.astype(jnp.float32).T.astype(jnp.int32)
    for at in range(0, rows, chunk):
        row = at + lax.broadcasted_iota(jnp.int32, (tokens, chunk), 1)
        gate = jnp.zeros((tokens, chunk), jnp.float32)
        for k in range(top):
            gate = jnp.where(row == target[:, k : k + 1], level[:, k : k + 1], gate)
        high = gate.astype(jnp.bfloat16)
        gates_ref[0, :, at : at + chunk] = high
        gates_ref[1, :, at : at + chunk] = (gate - high.astype(jnp.float32)).astype(jnp.bfloat16)
    copy.wait()


def prepare(target, levels, weight, rows):
    tokens = levels.shape[1]
    return pl.pallas_call(
        prepare_kernel,
        out_shape=(
            jax.ShapeDtypeStruct((2, tokens, rows), jnp.bfloat16),
            jax.ShapeDtypeStruct(weight.shape, jnp.bfloat16),
        ),
        in_specs=[WHOLE, WHOLE, FAR],
        out_specs=(WHOLE, WHOLE),
        scratch_shapes=[pltpu.VMEM((WIDE, tokens), jnp.float32), pltpu.SemaphoreType.DMA],
        compiler_params=pltpu.CompilerParams(vmem_limit_bytes=VMEM),
        cost_estimate=pl.CostEstimate(flops=4 << 20, bytes_accessed=8 << 20, transcendentals=0),
        name="prepare",
    )(target, levels, far(weight))


def combine_kernel(gates_ref, back_ref, out_ref):
    sources, _, lanes = back_ref.shape
    width = out_ref.shape[1]
    rows = sources * SLOTS
    tile = 2 * LANES
    row = lax.broadcasted_iota(jnp.int32, (sources, SLOTS, LANES), 1)
    unfolded = jnp.zeros((sources, SLOTS, LANES), jnp.float32)
    for j in range(SLOTS - 1):
        block = back_ref[:, :, j * LANES : (j + 1) * LANES].astype(jnp.float32)
        unfolded = jnp.where(row == j, block[:, SLOTS - 1 : SLOTS, :], unfolded)
    unfolded = unfolded.astype(jnp.bfloat16).reshape(rows, LANES)

    def gated(e, back):
        at = slice(e * rows, (e + 1) * rows)
        high = jnp.dot(gates_ref[0, :, at], back, preferred_element_type=jnp.float32)
        return high + jnp.dot(gates_ref[1, :, at], back, preferred_element_type=jnp.float32)

    for n in range(0, width, tile):
        first = back_ref[:, :, n : n + tile].reshape(rows, tile)
        at = width + n
        if at + tile <= lanes:
            second = back_ref[:, :, at : at + tile].reshape(rows, tile)
        else:
            second = jnp.concatenate(
                [back_ref[:, :, at : at + LANES].reshape(rows, LANES), unfolded], axis=1
            )
        total = gated(0, first) + gated(1, second)
        out_ref[:, n : n + tile] = (total * (1.0 / 1024.0)).astype(jnp.bfloat16)


def combine(gates, back):
    return pl.pallas_call(
        combine_kernel,
        out_shape=jax.ShapeDtypeStruct(
            (gates.shape[1], (back.shape[2] + LANES) // 2), jnp.bfloat16
        ),
        in_specs=[WHOLE, WHOLE],
        out_specs=WHOLE,
        compiler_params=pltpu.CompilerParams(vmem_limit_bytes=VMEM),
        name="combine",
    )(gates, back)


def shards(hidden_acts, picks, levels, down_weight):
    tokens, top = picks.shape
    half = hidden_acts.shape[-1]
    local, _, width = down_weight.shape
    devices = lax.axis_size("exp")
    experts = local * devices
    flat_hidden = jnp.transpose(hidden_acts, (1, 0, 2)).reshape(top * tokens, half)
    rows, target = route(picks.T, flat_hidden, experts)
    own = exchange(rows.reshape(devices, local * SLOTS, half))
    other = lax.ppermute(own, "head", [(0, 1), (1, 0)])
    head = lax.axis_index("head").astype(jnp.int32).reshape(1)
    gates, weight = prepare(target, levels.T, down_weight, experts * SLOTS)
    other, gates, weight = lax.optimization_barrier((other, gates, weight))
    outputs = run_experts(head, own, other, weight)
    back = exchange(outputs)
    return combine(gates, back)


def solution(mesh):
    placed = (
        P(("req", "exp"), None, "head"),
        P(("req", "exp"), None),
        P(("req", "exp"), None),
        P("exp", None, "head"),
    )
    return jax.shard_map(
        shards, mesh=mesh, in_specs=placed, out_specs=P(("req", "exp"), "head"), check_vma=False
    )
```

```python
import functools

import jax
import jax.numpy as jnp
from jax import lax
from jax.experimental import pallas as pl
from jax.experimental.pallas import tpu as pltpu
from jax.sharding import PartitionSpec as P

LANES = 128
RING = 8
STRIDE = 3
WIDE = 8
SLOTS = 16
VMEM = 24 * 1024 * 1024
WHOLE = pl.BlockSpec(memory_space=pltpu.VMEM)
FAR = pl.BlockSpec(memory_space=pltpu.HBM)


def placed(expert):
    device, own = expert // 2, expert % 2
    z, y = device // RING, device % RING
    return (z * RING + (y + (RING - 1) * z) * STRIDE % RING) * 2 + own


def exchange(array):
    order = [z * RING + (z + y * STRIDE) % RING for z in range(RING) for y in range(RING)]
    return lax.all_to_all(
        array, "exp", split_axis=0, concat_axis=0, tiled=True, axis_index_groups=[order]
    )


def far(array):
    return pltpu.with_memory_space_constraint(array, pltpu.HBM)


def route_kernel(
    picks_far, hidden_far, rows_ref, target_ref, pick_ref, hidden_ref, pick_sem, hidden_sem, *, experts
):
    pick_copy = pltpu.make_async_copy(picks_far, pick_ref, pick_sem)
    hidden_copy = pltpu.make_async_copy(hidden_far, hidden_ref, hidden_sem)
    pick_copy.start()
    hidden_copy.start()
    pick_copy.wait()
    top, tokens = pick_ref.shape
    before = lax.broadcasted_iota(jnp.int32, (tokens, tokens), 0)
    after = lax.broadcasted_iota(jnp.int32, (tokens, tokens), 1)
    earlier = jnp.where(before < after, 1.0, 0.0).astype(jnp.bfloat16)
    named = lax.broadcasted_iota(jnp.int32, (experts, tokens), 0)
    carry = jnp.zeros((experts, 1), jnp.float32)
    target_ref[...] = jnp.full(target_ref.shape, -1, jnp.int32)
    targets = []
    for k in range(top):
        pick = pick_ref[k : k + 1, :]
        onehot = jnp.where(named == pick, 1.0, 0.0)
        count = jnp.dot(
            onehot.astype(jnp.bfloat16), earlier, preferred_element_type=jnp.float32
        )
        slot = jnp.sum(onehot * (count + carry), axis=0, keepdims=True)
        carry = carry + jnp.sum(onehot, axis=1, keepdims=True)
        targets.append(placed(pick) * SLOTS + slot.astype(jnp.int32))
        target_ref[k : k + 1, :] = targets[k]
    hidden_copy.wait()
    chunk = 256
    for at in range(0, rows_ref.shape[0], chunk):
        row = at + lax.broadcasted_iota(jnp.int32, (chunk, tokens), 0)
        chosen = jnp.concatenate(
            [jnp.where(row == target, 1.0, 0.0).astype(jnp.bfloat16) for target in targets], axis=1
        )
        rows_ref[at : at + chunk, :] = jnp.dot(
            chosen, hidden_ref[...], preferred_element_type=jnp.float32
        ).astype(jnp.bfloat16)


def route(picks, hidden, experts):
    return pl.pallas_call(
        functools.partial(route_kernel, experts=experts),
        out_shape=(
            jax.ShapeDtypeStruct((experts * SLOTS, hidden.shape[1]), jnp.bfloat16),
            jax.ShapeDtypeStruct((WIDE, picks.shape[1]), jnp.int32),
        ),
        in_specs=[FAR, FAR],
        out_specs=(WHOLE, WHOLE),
        scratch_shapes=[
            pltpu.VMEM(picks.shape, jnp.int32),
            pltpu.VMEM(hidden.shape, jnp.bfloat16),
            pltpu.SemaphoreType.DMA,
            pltpu.SemaphoreType.DMA,
        ],
        compiler_params=pltpu.CompilerParams(vmem_limit_bytes=VMEM),
        name="route",
    )(far(picks), far(hidden))


def expert_kernel(head_ref, own_ref, other_ref, weight_ref, out_ref):
    sources, _, half = own_ref.shape
    width = weight_ref.shape[2]
    first = head_ref[0] == 0
    last_row = lax.broadcasted_iota(jnp.int32, (sources, SLOTS, LANES), 1) == SLOTS - 1
    tile = 2 * LANES
    parts = width // tile

    def halves(e):
        at = slice(e * SLOTS, (e + 1) * SLOTS)
        own = own_ref[:, at, :].reshape(sources * SLOTS, half)
        other = other_ref[:, at, :].reshape(sources * SLOTS, half)
        return jnp.concatenate(
            [jnp.where(first, own, other), jnp.where(first, other, own)], axis=1
        )

    def product(whole, e, n):
        total = jnp.dot(
            whole, weight_ref[e, :, n * tile : (n + 1) * tile], preferred_element_type=jnp.float32
        )
        return [total[:, i * LANES : (i + 1) * LANES].reshape(sources, SLOTS, LANES) for i in (0, 1)]

    def put(j, block):
        if j < SLOTS - 1:
            block = jnp.where(last_row, folded[:, j : j + 1, :], block)
        out_ref[:, :, j * LANES : (j + 1) * LANES] = block.astype(jnp.bfloat16)

    whole = halves(1)
    left, folded = product(whole, 1, parts - 1)
    put(4 * parts - 2, left)
    for n in range(parts - 1):
        for i, block in enumerate(product(whole, 1, n)):
            put(2 * (parts + n) + i, block)
    whole = halves(0)
    for n in range(parts):
        for i, block in enumerate(product(whole, 0, n)):
            put(2 * n + i, block)


def run_experts(head, own, other, weight):
    sources, rows, half = own.shape
    local, depth, width = weight.shape
    assert local == 2 and width % (2 * LANES) == 0 and 2 * width >= SLOTS * LANES
    return pl.pallas_call(
        expert_kernel,
        out_shape=jax.ShapeDtypeStruct((sources, SLOTS, 2 * width - LANES), jnp.bfloat16),
        in_specs=[pl.BlockSpec(memory_space=pltpu.SMEM), WHOLE, WHOLE, WHOLE],
        out_specs=WHOLE,
        compiler_params=pltpu.CompilerParams(vmem_limit_bytes=VMEM),
        cost_estimate=pl.CostEstimate(
            flops=2 * sources * rows * depth * width, bytes_accessed=12 << 20, transcendentals=0
        ),
        name="experts",
    )(head, own, other, weight)


def prepare_kernel(target_ref, level_ref, weight_hbm, gates_ref, weight_ref, wide_ref, sem):
    copy = pltpu.make_async_copy(weight_hbm, weight_ref, sem)
    copy.start()
    tokens, rows = gates_ref.shape[1:]
    top = level_ref.shape[0]
    chunk = 256
    wide_ref[...] = jnp.zeros_like(wide_ref)
    wide_ref[0:top, :] = level_ref[...].astype(jnp.float32)
    level = wide_ref[...].T
    row_of = target_ref[...]
    row_of = (
        ((row_of // SLOTS) % 2) * (rows // 2) + (row_of // (2 * SLOTS)) * SLOTS + row_of % SLOTS
    )
    target = row_of.astype(jnp.float32).T.astype(jnp.int32)
    for at in range(0, rows, chunk):
        row = at + lax.broadcasted_iota(jnp.int32, (tokens, chunk), 1)
        gate = jnp.zeros((tokens, chunk), jnp.float32)
        for k in range(top):
            gate = jnp.where(row == target[:, k : k + 1], level[:, k : k + 1], gate)
        high = gate.astype(jnp.bfloat16)
        gates_ref[0, :, at : at + chunk] = high
        gates_ref[1, :, at : at + chunk] = (gate - high.astype(jnp.float32)).astype(jnp.bfloat16)
    copy.wait()


def prepare(target, levels, weight, rows):
    tokens = levels.shape[1]
    return pl.pallas_call(
        prepare_kernel,
        out_shape=(
            jax.ShapeDtypeStruct((2, tokens, rows), jnp.bfloat16),
            jax.ShapeDtypeStruct(weight.shape, jnp.bfloat16),
        ),
        in_specs=[WHOLE, WHOLE, FAR],
        out_specs=(WHOLE, WHOLE),
        scratch_shapes=[pltpu.VMEM((WIDE, tokens), jnp.float32), pltpu.SemaphoreType.DMA],
        compiler_params=pltpu.CompilerParams(vmem_limit_bytes=VMEM),
        cost_estimate=pl.CostEstimate(flops=4 << 20, bytes_accessed=8 << 20, transcendentals=0),
        name="prepare",
    )(target, levels, far(weight))


def combine_kernel(gates_ref, back_ref, out_ref):
    sources, _, lanes = back_ref.shape
    width = out_ref.shape[1]
    rows = sources * SLOTS
    tile = 2 * LANES
    row = lax.broadcasted_iota(jnp.int32, (sources, SLOTS, LANES), 1)
    unfolded = jnp.zeros((sources, SLOTS, LANES), jnp.float32)
    for j in range(SLOTS - 1):
        block = back_ref[:, :, j * LANES : (j + 1) * LANES].astype(jnp.float32)
        unfolded = jnp.where(row == j, block[:, SLOTS - 1 : SLOTS, :], unfolded)
    unfolded = unfolded.astype(jnp.bfloat16).reshape(rows, LANES)

    def gated(e, back):
        at = slice(e * rows, (e + 1) * rows)
        high = jnp.dot(gates_ref[0, :, at], back, preferred_element_type=jnp.float32)
        return high + jnp.dot(gates_ref[1, :, at], back, preferred_element_type=jnp.float32)

    for n in range(0, width, tile):
        first = back_ref[:, :, n : n + tile].reshape(rows, tile)
        at = width + n
        if at + tile <= lanes:
            second = back_ref[:, :, at : at + tile].reshape(rows, tile)
        else:
            second = jnp.concatenate(
                [back_ref[:, :, at : at + LANES].reshape(rows, LANES), unfolded], axis=1
            )
        total = gated(0, first) + gated(1, second)
        out_ref[:, n : n + tile] = (total * (1.0 / 1024.0)).astype(jnp.bfloat16)


def combine(gates, back):
    return pl.pallas_call(
        combine_kernel,
        out_shape=jax.ShapeDtypeStruct(
            (gates.shape[1], (back.shape[2] + LANES) // 2), jnp.bfloat16
        ),
        in_specs=[WHOLE, WHOLE],
        out_specs=WHOLE,
        compiler_params=pltpu.CompilerParams(vmem_limit_bytes=VMEM),
        name="combine",
    )(gates, back)


def shards(hidden_acts, picks, levels, down_weight):
    tokens, top = picks.shape
    half = hidden_acts.shape[-1]
    local, _, width = down_weight.shape
    devices = lax.axis_size("exp")
    experts = local * devices
    flat_hidden = jnp.transpose(hidden_acts, (1, 0, 2)).reshape(top * tokens, half)
    rows, target = route(picks.T, flat_hidden, experts)
    own = exchange(rows.reshape(devices, local * SLOTS, half))
    other = lax.ppermute(own, "head", [(0, 1), (1, 0)])
    head = lax.axis_index("head").astype(jnp.int32).reshape(1)
    gates, weight = prepare(target, levels.T, down_weight, experts * SLOTS)
    other, gates, weight = lax.optimization_barrier((other, gates, weight))
    outputs = run_experts(head, own, other, weight)
    back = exchange(outputs)
    return combine(gates, back)


def solution(mesh):
    placed = (
        P(("req", "exp"), None, "head"),
        P(("req", "exp"), None),
        P(("req", "exp"), None),
        P("exp", None, "head"),
    )
    return jax.shard_map(
        shards, mesh=mesh, in_specs=placed, out_specs=P(("req", "exp"), "head"), check_vma=False
    )
```

```python
import functools

import jax
import jax.numpy as jnp
from jax import lax
from jax.experimental import pallas as pl
from jax.experimental.pallas import tpu as pltpu
from jax.sharding import PartitionSpec as P

LANES = 128
RING = 8
STRIDE = 3
WIDE = 8
SLOTS = 16
VMEM = 24 * 1024 * 1024
WHOLE = pl.BlockSpec(memory_space=pltpu.VMEM)
FAR = pl.BlockSpec(memory_space=pltpu.HBM)


def placed(expert):
    device, own = expert // 2, expert % 2
    return (device // RING * RING + device * STRIDE % RING) * 2 + own


def exchange(array):
    order = [z + y * STRIDE % RING for z in range(0, array.shape[0], RING) for y in range(RING)]
    return lax.all_to_all(
        array, "exp", split_axis=0, concat_axis=0, tiled=True, axis_index_groups=[order]
    )


def far(array):
    return pltpu.with_memory_space_constraint(array, pltpu.HBM)


def route_kernel(
    picks_far, hidden_far, rows_ref, target_ref, pick_ref, hidden_ref, pick_sem, hidden_sem, *, experts
):
    pick_copy = pltpu.make_async_copy(picks_far, pick_ref, pick_sem)
    hidden_copy = pltpu.make_async_copy(hidden_far, hidden_ref, hidden_sem)
    pick_copy.start()
    hidden_copy.start()
    pick_copy.wait()
    top, tokens = pick_ref.shape
    before = lax.broadcasted_iota(jnp.int32, (tokens, tokens), 0)
    after = lax.broadcasted_iota(jnp.int32, (tokens, tokens), 1)
    earlier = jnp.where(before < after, 1.0, 0.0).astype(jnp.bfloat16)
    named = lax.broadcasted_iota(jnp.int32, (experts, tokens), 0)
    carry = jnp.zeros((experts, 1), jnp.float32)
    target_ref[...] = jnp.full(target_ref.shape, -1, jnp.int32)
    targets = []
    for k in range(top):
        pick = pick_ref[k : k + 1, :]
        onehot = jnp.where(named == pick, 1.0, 0.0)
        count = jnp.dot(
            onehot.astype(jnp.bfloat16), earlier, preferred_element_type=jnp.float32
        )
        slot = jnp.sum(onehot * (count + carry), axis=0, keepdims=True)
        carry = carry + jnp.sum(onehot, axis=1, keepdims=True)
        targets.append(placed(pick) * SLOTS + slot.astype(jnp.int32))
        target_ref[k : k + 1, :] = targets[k]
    hidden_copy.wait()
    chunk = 256
    for at in range(0, rows_ref.shape[0], chunk):
        row = at + lax.broadcasted_iota(jnp.int32, (chunk, tokens), 0)
        chosen = jnp.concatenate(
            [jnp.where(row == target, 1.0, 0.0).astype(jnp.bfloat16) for target in targets], axis=1
        )
        rows_ref[at : at + chunk, :] = jnp.dot(
            chosen, hidden_ref[...], preferred_element_type=jnp.float32
        ).astype(jnp.bfloat16)


def route(picks, hidden, experts):
    return pl.pallas_call(
        functools.partial(route_kernel, experts=experts),
        out_shape=(
            jax.ShapeDtypeStruct((experts * SLOTS, hidden.shape[1]), jnp.bfloat16),
            jax.ShapeDtypeStruct((WIDE, picks.shape[1]), jnp.int32),
        ),
        in_specs=[FAR, FAR],
        out_specs=(WHOLE, WHOLE),
        scratch_shapes=[
            pltpu.VMEM(picks.shape, jnp.int32),
            pltpu.VMEM(hidden.shape, jnp.bfloat16),
            pltpu.SemaphoreType.DMA,
            pltpu.SemaphoreType.DMA,
        ],
        compiler_params=pltpu.CompilerParams(vmem_limit_bytes=VMEM),
        name="route",
    )(far(picks), far(hidden))


def expert_kernel(head_ref, own_ref, other_ref, weight_ref, out_ref):
    sources, _, half = own_ref.shape
    width = weight_ref.shape[2]
    first = head_ref[0] == 0
    last_row = lax.broadcasted_iota(jnp.int32, (sources, SLOTS, LANES), 1) == SLOTS - 1
    tile = 2 * LANES
    parts = width // tile

    def halves(e):
        at = slice(e * SLOTS, (e + 1) * SLOTS)
        own = own_ref[:, at, :].reshape(sources * SLOTS, half)
        other = other_ref[:, at, :].reshape(sources * SLOTS, half)
        return jnp.concatenate(
            [jnp.where(first, own, other), jnp.where(first, other, own)], axis=1
        )

    def product(whole, e, n):
        total = jnp.dot(
            whole, weight_ref[e, :, n * tile : (n + 1) * tile], preferred_element_type=jnp.float32
        )
        return [total[:, i * LANES : (i + 1) * LANES].reshape(sources, SLOTS, LANES) for i in (0, 1)]

    def put(j, block):
        if j < SLOTS - 1:
            block = jnp.where(last_row, folded[:, j : j + 1, :], block)
        out_ref[:, :, j * LANES : (j + 1) * LANES] = block.astype(jnp.bfloat16)

    whole = halves(1)
    left, folded = product(whole, 1, parts - 1)
    put(4 * parts - 2, left)
    for n in range(parts - 1):
        for i, block in enumerate(product(whole, 1, n)):
            put(2 * (parts + n) + i, block)
    whole = halves(0)
    for n in range(parts):
        for i, block in enumerate(product(whole, 0, n)):
            put(2 * n + i, block)


def run_experts(head, own, other, weight):
    sources, rows, half = own.shape
    local, depth, width = weight.shape
    assert local == 2 and width % (2 * LANES) == 0 and 2 * width >= SLOTS * LANES
    return pl.pallas_call(
        expert_kernel,
        out_shape=jax.ShapeDtypeStruct((sources, SLOTS, 2 * width - LANES), jnp.bfloat16),
        in_specs=[pl.BlockSpec(memory_space=pltpu.SMEM), WHOLE, WHOLE, WHOLE],
        out_specs=WHOLE,
        compiler_params=pltpu.CompilerParams(vmem_limit_bytes=VMEM),
        cost_estimate=pl.CostEstimate(
            flops=2 * sources * rows * depth * width, bytes_accessed=12 << 20, transcendentals=0
        ),
        name="experts",
    )(head, own, other, weight)


def prepare_kernel(target_ref, level_ref, weight_hbm, gates_ref, weight_ref, wide_ref, sem):
    copy = pltpu.make_async_copy(weight_hbm, weight_ref, sem)
    copy.start()
    tokens, rows = gates_ref.shape[1:]
    top = level_ref.shape[0]
    chunk = 256
    wide_ref[...] = jnp.zeros_like(wide_ref)
    wide_ref[0:top, :] = level_ref[...].astype(jnp.float32)
    level = wide_ref[...].T
    row_of = target_ref[...]
    row_of = (
        ((row_of // SLOTS) % 2) * (rows // 2) + (row_of // (2 * SLOTS)) * SLOTS + row_of % SLOTS
    )
    target = row_of.astype(jnp.float32).T.astype(jnp.int32)
    for at in range(0, rows, chunk):
        row = at + lax.broadcasted_iota(jnp.int32, (tokens, chunk), 1)
        gate = jnp.zeros((tokens, chunk), jnp.float32)
        for k in range(top):
            gate = jnp.where(row == target[:, k : k + 1], level[:, k : k + 1], gate)
        high = gate.astype(jnp.bfloat16)
        gates_ref[0, :, at : at + chunk] = high
        gates_ref[1, :, at : at + chunk] = (gate - high.astype(jnp.float32)).astype(jnp.bfloat16)
    copy.wait()


def prepare(target, levels, weight, rows):
    tokens = levels.shape[1]
    return pl.pallas_call(
        prepare_kernel,
        out_shape=(
            jax.ShapeDtypeStruct((2, tokens, rows), jnp.bfloat16),
            jax.ShapeDtypeStruct(weight.shape, jnp.bfloat16),
        ),
        in_specs=[WHOLE, WHOLE, FAR],
        out_specs=(WHOLE, WHOLE),
        scratch_shapes=[pltpu.VMEM((WIDE, tokens), jnp.float32), pltpu.SemaphoreType.DMA],
        compiler_params=pltpu.CompilerParams(vmem_limit_bytes=VMEM),
        cost_estimate=pl.CostEstimate(flops=4 << 20, bytes_accessed=8 << 20, transcendentals=0),
        name="prepare",
    )(target, levels, far(weight))


def combine_kernel(gates_ref, back_ref, out_far, out_ref, sems):
    sources, _, lanes = back_ref.shape
    width = out_ref.shape[1]
    rows = sources * SLOTS
    tile = 2 * LANES
    parts = width // tile
    row = lax.broadcasted_iota(jnp.int32, (sources, SLOTS, LANES), 1)
    unfolded = jnp.zeros((sources, SLOTS, LANES), jnp.float32)
    share = -(-(SLOTS - 1) // (parts - 1))
    copies = []

    def gated(e, back):
        at = slice(e * rows, (e + 1) * rows)
        high = jnp.dot(gates_ref[0, :, at], back, preferred_element_type=jnp.float32)
        return high + jnp.dot(gates_ref[1, :, at], back, preferred_element_type=jnp.float32)

    for n in range(parts):
        first = back_ref[:, :, n * tile : (n + 1) * tile].reshape(rows, tile)
        at = width + n * tile
        if n < parts - 1:
            second = back_ref[:, :, at : at + tile].reshape(rows, tile)
        else:
            second = jnp.concatenate(
                [
                    back_ref[:, :, at : at + LANES].reshape(rows, LANES),
                    unfolded.astype(jnp.bfloat16).reshape(rows, LANES),
                ],
                axis=1,
            )
        total = gated(0, first) + gated(1, second)
        to = slice(n * tile, (n + 1) * tile)
        out_ref[:, to] = (total * (1.0 / 1024.0)).astype(jnp.bfloat16)
        copies.append(pltpu.make_async_copy(out_ref.at[:, to], out_far.at[:, to], sems.at[n]))
        copies[n].start()
        for j in range(n * share, min((n + 1) * share, SLOTS - 1)):
            block = back_ref[:, :, j * LANES : (j + 1) * LANES].astype(jnp.float32)
            unfolded = jnp.where(row == j, block[:, SLOTS - 1 : SLOTS, :], unfolded)
    for copy in copies:
        copy.wait()


def combine(gates, back):
    tokens = gates.shape[1]
    width = (back.shape[2] + LANES) // 2
    return pl.pallas_call(
        combine_kernel,
        out_shape=jax.ShapeDtypeStruct((tokens, width), jnp.bfloat16),
        in_specs=[WHOLE, WHOLE],
        out_specs=FAR,
        scratch_shapes=[
            pltpu.VMEM((tokens, width), jnp.bfloat16),
            pltpu.SemaphoreType.DMA((width // (2 * LANES),)),
        ],
        compiler_params=pltpu.CompilerParams(vmem_limit_bytes=VMEM),
        name="combine",
    )(gates, back)


def shards(hidden_acts, picks, levels, down_weight):
    tokens, top = picks.shape
    half = hidden_acts.shape[-1]
    local, _, width = down_weight.shape
    devices = lax.axis_size("exp")
    experts = local * devices
    flat_hidden = jnp.transpose(hidden_acts, (1, 0, 2)).reshape(top * tokens, half)
    rows, target = route(picks.T, flat_hidden, experts)
    own = exchange(rows.reshape(devices, local * SLOTS, half))
    other = lax.ppermute(own, "head", [(0, 1), (1, 0)])
    head = lax.axis_index("head").astype(jnp.int32).reshape(1)
    gates, weight = prepare(target, levels.T, down_weight, experts * SLOTS)
    other, gates, weight = lax.optimization_barrier((other, gates, weight))
    outputs = run_experts(head, own, other, weight)
    back = exchange(outputs)
    return combine(gates, back)


def solution(mesh):
    placed = (
        P(("req", "exp"), None, "head"),
        P(("req", "exp"), None),
        P(("req", "exp"), None),
        P("exp", None, "head"),
    )
    return jax.shard_map(
        shards, mesh=mesh, in_specs=placed, out_specs=P(("req", "exp"), "head"), check_vma=False
    )
```
